512 devices in a mesh: replica: 16 (over z_lo, y), fsdp: 32 (over x, z_hi, core).
Axes of the slice: x: 4, y: 8, z: 8 (z_hi: 4, z_lo: 2; z = z_hi * 2 + z_lo), core: 2. Of those that a mesh axis runs over, the one named last changes fastest.
Arguments:
- activations: bfloat16 [131072, 4096], P(('replica', 'fsdp')), may hold values from -6 to 6
- cotangent: bfloat16 [131072, 512], P(('replica', 'fsdp')), may hold values from -6 to 6
- local_weight: float32 [16, 4096, 512], P('replica', 'fsdp'), may hold values from -6 to 6
- first_moment: float32 [16, 4096, 512], P('replica', 'fsdp'), may hold values from -4 to 4
- second_moment: float32 [16, 4096, 512], P('replica', 'fsdp'), may hold values from 0.25 to 4
- anchor_weight: float32 [4096, 512], P('fsdp'), may hold values from -6 to 6
- outer_momentum: float32 [4096, 512], P('fsdp'), may hold values from -3 to 3
Outputs:
- key_out: bfloat16 [131072, 512], P(('replica', 'fsdp'))
- new_weight: float32 [16, 4096, 512], P('replica', 'fsdp')
- new_first: float32 [16, 4096, 512], P('replica', 'fsdp')
- new_second: float32 [16, 4096, 512], P('replica', 'fsdp')
- new_anchor: float32 [4096, 512], P('fsdp')
- new_momentum: float32 [4096, 512], P('fsdp')
The draws below stay inside these ranges and needn't reach their ends.
All inputs are finite; a program needn't handle non-finite values.
Results may differ from the reference program's by a relative error of at most 0.012.
Values may be sent and summed in bfloat16 or wider, within the bound.
No kernel may reach another device: no remote copies, remote signals or barrier semaphores. Data moves between devices by JAX's collectives and lax.ppermute only.
A program may use at most 64 MiB of HBM per device.

```python
import math
import jax
import jax.numpy as jnp
from jax import lax

DWIN = 4096
KVW = 512
TOK_DEV = 256
TOK_REP = 8192
TOKENS = 131072
N_REPLICA = 16
N_FSDP = 32


def levels(key, shape, pieces, smallest, largest):
    level = 1.0
    for position, blocks in pieces:
        steps = jax.random.uniform(jax.random.fold_in(jax.random.fold_in(key, 6), position), (blocks,), jnp.float32, smallest / len(pieces), largest / len(pieces))
        level = level * jnp.repeat(jnp.exp(steps), shape[position] // blocks).reshape((-1,) + (1,) * (len(shape) - 1 - position))
    return level


def scatter_about(rng, shape, scale, bound, shards=(), held_as=jnp.bfloat16):
    drawn = scale * jax.random.normal(rng, shape, jnp.float32)
    if shards:
        drawn = drawn * levels(rng, shape, shards, -0.22, 0.18)
    return jnp.clip(drawn, -bound, bound).astype(held_as)


def setup_inputs(seed: int = 0) -> dict:
    streams_of = jax.random.split(jax.random.key(seed), 8)
    activations = scatter_about(streams_of[0], (TOKENS, DWIN), 1.0, 6.0, ((0, 512),))
    cotangent = scatter_about(streams_of[1], (TOKENS, KVW), 1.0, 6.0, ((0, 512),))
    local_weight = scatter_about(streams_of[2], (N_REPLICA, DWIN, KVW), 1.0, 6.0, ((0, 16), (1, 32)), jnp.float32)
    first_moment = scatter_about(streams_of[3], (N_REPLICA, DWIN, KVW), 0.5, 4.0, ((0, 16), (1, 32)), jnp.float32)
    second_moment = jnp.clip(jnp.exp(math.log(4.0) - 2.7725887 * jax.random.uniform(streams_of[4], (N_REPLICA, DWIN, KVW), jnp.float32) ** levels(streams_of[4], (N_REPLICA, DWIN, KVW), ((0, 16), (1, 32)), -0.2, 0.2)), 0.25, 4.0)
    anchor_weight = scatter_about(streams_of[5], (DWIN, KVW), 1.0, 6.0, ((0, 32),), jnp.float32)
    outer_momentum = scatter_about(streams_of[6], (DWIN, KVW), 0.3, 3.0, ((0, 32),), jnp.float32)
    return dict(activations=activations, cotangent=cotangent, local_weight=local_weight, first_moment=first_moment, second_moment=second_moment, anchor_weight=anchor_weight, outer_momentum=outer_momentum)


def replica_keys(pair):
    inputs, weight = pair
    keys = jnp.dot(inputs, weight.astype(jnp.bfloat16), preferred_element_type=jnp.float32)
    return (keys * DWIN ** (-0.5)).astype(jnp.bfloat16)

def replica_grad(pair):
    inputs, grads = pair
    blocks_in = inputs.reshape(N_FSDP, TOK_DEV, DWIN)
    blocks_grad = grads.reshape(N_FSDP, TOK_DEV, KVW)

    def add_block(total, block):
        term = lax.dot_general(block[0], block[1], (((0,), (0,)), ((), ())), preferred_element_type=jnp.float32)
        rounded = lax.optimization_barrier(term.astype(jnp.bfloat16))
        return (total + rounded.astype(jnp.float32), None)
    start = jnp.zeros((DWIN, KVW), jnp.float32)
    total, unused = lax.scan(add_block, start, (blocks_in, blocks_grad))
    return total * DWIN ** (-0.5)

def reference(activations, cotangent, local_weight, first_moment, second_moment, anchor_weight, outer_momentum):
    inputs = activations.reshape(N_REPLICA, TOK_REP, DWIN)
    grads = cotangent.reshape(N_REPLICA, TOK_REP, KVW)
    key_out = lax.map(replica_keys, (inputs, local_weight)).reshape(TOKENS, KVW)
    grad = lax.map(replica_grad, (inputs, grads))
    new_first = 0.9 * first_moment + 0.1 * grad
    new_second = 0.95 * second_moment + 0.05 * grad * grad
    stepped = local_weight - 0.02 * (new_first / (jnp.sqrt(new_second) + 1e-08) + 0.1 * local_weight)
    pseudo = anchor_weight - lax.optimization_barrier(jnp.sum(local_weight, axis=0)) * (1.0 / N_REPLICA)
    new_momentum = 0.9 * outer_momentum + pseudo
    new_anchor = anchor_weight - 0.7 * (pseudo + 0.9 * new_momentum)
    new_weight = 0.5 * stepped + 0.5 * new_anchor[None]
    return (key_out, new_weight, new_first, new_second, new_anchor, new_momentum)
```

```python
import jax
import jax.numpy as jnp
from jax import lax
from jax.sharding import Mesh, PartitionSpec as P

REPLICA = ("zl", "y")
FSDP = ("x", "zh", "core")
F32 = jnp.float32
BF16 = jnp.bfloat16


def outer_update(summed, anchor_part, momentum_part, replicas):
    pseudo = anchor_part - summed * (1.0 / replicas)
    momentum_next = 0.9 * momentum_part + pseudo
    anchor_next = anchor_part - 0.7 * (pseudo + 0.9 * momentum_next)
    return (anchor_next, momentum_next)


def exchange(blocks, axis):
    return lax.all_to_all(blocks, axis, 0, 0, tiled=True)


def gather(block, axis):
    count = lax.axis_size(axis)
    return exchange(jnp.broadcast_to(block[None], (count,) + block.shape), axis)


def total(blocks):
    return jnp.sum(blocks.astype(F32), axis=0)


def swap(block):
    return lax.ppermute(block, "core", [(0, 1), (1, 0)])


def columns_of(x, parity):
    tokens, width = x.shape
    pairs = [
        lax.select(
            parity == 0, x[:, at : at + 128], x[:, at + 128 : at + 256]
        )
        for at in range(0, width, 256)
    ]
    return jnp.concatenate(pairs, axis=1)


def shards(
    activations, cotangent, local_weight, first_moment, second_moment, anchor_weight, outer_momentum
):
    tokens, width = activations.shape
    rows, features = anchor_weight.shape
    scale_factor = width ** (-0.5)
    core = lax.axis_index("core")
    weight = local_weight[0]
    weight_half = weight.astype(BF16)

    theirs = swap(columns_of(activations, 1 - core))
    their_cotangent = swap(cotangent)
    mine = columns_of(activations, core)

    column = gather(weight_half, "zh").reshape(-1, features)
    half = gather(column, "x").reshape(-1, features)

    term = lax.dot_general(
        jnp.concatenate([mine, theirs], axis=0),
        jnp.concatenate([cotangent, their_cotangent], axis=0),
        (((0,), (0,)), ((), ())),
        preferred_element_type=F32,
    ).astype(BF16)
    part = total(exchange(term.reshape(4, -1, features), "x")).astype(BF16)
    grad_sum = total(exchange(part.reshape(4, rows, features), "zh"))
    grad = grad_sum * scale_factor

    replicas = lax.axis_size(REPLICA)
    pieces = exchange(weight_half.reshape(replicas, -1, features), REPLICA)
    summed = gather(total(pieces).astype(BF16), REPLICA).reshape(rows, features).astype(F32)

    their_keys = swap(jnp.dot(theirs, half, preferred_element_type=F32))
    keys = jnp.dot(mine, half, preferred_element_type=F32) + their_keys
    key_out = (keys * scale_factor).astype(BF16)

    new_first = 0.9 * first_moment[0] + 0.1 * grad
    new_second = 0.95 * second_moment[0] + 0.05 * grad * grad
    stepped = weight - 0.02 * (new_first / (jnp.sqrt(new_second) + 1e-08) + 0.1 * weight)
    new_anchor, new_momentum = outer_update(summed, anchor_weight, outer_momentum, replicas)
    new_weight = 0.5 * stepped + 0.5 * new_anchor
    return (key_out, new_weight[None], new_first[None], new_second[None], new_anchor, new_momentum)


def solution(mesh):
    fine = Mesh(mesh.devices.reshape(2, 8, 4, 4, 2), REPLICA + FSDP)
    return jax.shard_map(
        shards,
        mesh=fine,
        in_specs=(
            P(REPLICA + FSDP, None),
            P(REPLICA + FSDP, None),
            P(REPLICA, FSDP, None),
            P(REPLICA, FSDP, None),
            P(REPLICA, FSDP, None),
            P(FSDP, None),
            P(FSDP, None),
        ),
        out_specs=(
            P(REPLICA + FSDP, None),
            P(REPLICA, FSDP, None),
            P(REPLICA, FSDP, None),
            P(REPLICA, FSDP, None),
            P(FSDP, None),
            P(FSDP, None),
        ),
        check_vma=False,
    )
```

```python
import jax
import jax.numpy as jnp
from jax import lax
from jax.experimental import pallas as pl
from jax.experimental.pallas import tpu as pltpu
from jax.sharding import Mesh, PartitionSpec as P

REPLICA = ("zl", "y")
FSDP = ("x", "zh", "core")
F32 = jnp.float32
BF16 = jnp.bfloat16
BLOCK = 128
SMEM = pl.BlockSpec(memory_space=pltpu.SMEM)
VMEM = pl.BlockSpec(memory_space=pltpu.VMEM)


def outer_update(summed, anchor_part, momentum_part, replicas):
    pseudo = anchor_part - summed * (1.0 / replicas)
    momentum_next = 0.9 * momentum_part + pseudo
    anchor_next = anchor_part - 0.7 * (pseudo + 0.9 * momentum_next)
    return (anchor_next, momentum_next)


def trade(block, axis, mask):
    return lax.ppermute(block, axis, [(i, i ^ mask) for i in range(lax.axis_size(axis))])


def add_other(value, axis, mask):
    held = value.astype(BF16)
    return held.astype(F32) + trade(held, axis, mask).astype(F32)


def exchange(blocks, axis):
    return lax.all_to_all(blocks, axis, 0, 0, tiled=True)


def total(blocks):
    return jnp.sum(blocks.astype(F32), axis=0)


def call(kernel, outs, args, flops, name):
    moved = sum(a.size * a.dtype.itemsize for a in args)
    return pl.pallas_call(
        kernel,
        in_specs=[SMEM] + [VMEM] * (len(args) - 1),
        out_specs=[VMEM] * len(outs),
        out_shape=outs,
        cost_estimate=pl.CostEstimate(flops=flops, bytes_accessed=2 * moved, transcendentals=0),
        compiler_params=pltpu.CompilerParams(vmem_limit_bytes=24 * 2**20),
        name=name,
    )(*args)


def send_kernel(place_ref, x_ref, c_ref, out_ref):
    width = x_ref.shape[1]

    def put(offset):
        for block in range(width // (2 * BLOCK)):
            at = 2 * BLOCK * block + offset
            out_ref[:, BLOCK * block : BLOCK * (block + 1)] = x_ref[:, at : at + BLOCK]

    pl.when(place_ref[0] == 0)(lambda: put(BLOCK))
    pl.when(place_ref[0] != 0)(lambda: put(0))
    out_ref[:, width // 2 :] = c_ref[...]


def own_block(core, x_ref, at):
    return x_ref[:, pl.ds(pl.multiple_of((2 * at + core) * BLOCK, BLOCK), BLOCK)]


def their_block(core, got_ref, at):
    return got_ref[:, pl.ds(pl.multiple_of(at * BLOCK, BLOCK), BLOCK)]


def four_blocks(pick, core, ref, j):
    return jnp.concatenate([pick(core, ref, 4 * j + k) for k in range(4)], axis=1)


def grad_kernel(place_ref, x_ref, c_ref, got_ref, out_ref):
    ours = c_ref[...]
    theirs = got_ref[:, got_ref.shape[1] - ours.shape[1] :]
    rows = (((0,), (0,)), ((), ()))
    for j in range(4):
        a = four_blocks(own_block, place_ref[0], x_ref, j)
        b = four_blocks(their_block, place_ref[0], got_ref, j)
        term = lax.dot_general(a, ours, rows, preferred_element_type=F32)
        term += lax.dot_general(b, theirs, rows, preferred_element_type=F32)
        out_ref[j] = term.astype(out_ref.dtype)


def keys_kernel(pick, place_ref, x_ref, *refs):
    out_ref = refs[-1]
    for j, w_ref in enumerate(refs[:-1]):
        group = 4 * (place_ref[1] ^ j)
        picked = [pick(place_ref[0], x_ref, group + (place_ref[2] ^ k)) for k in range(4)]
        a = jnp.concatenate(picked, axis=1)
        term = jnp.dot(a, w_ref[...], preferred_element_type=F32)
        out_ref[...] = term if j == 0 else out_ref[...] + term


def shards(
    activations, cotangent, local_weight, first_moment, second_moment, anchor_weight, outer_momentum
):
    tokens, width = activations.shape
    rows, features = anchor_weight.shape
    scale_factor = width ** (-0.5)
    weight = local_weight[0]
    weight_half = weight.astype(BF16)
    place = jnp.stack([lax.axis_index(a) for a in ("core", "x", "zh")]).astype(jnp.int32)
    keys_shape = jax.ShapeDtypeStruct((tokens, features), F32)
    term_shape = jax.ShapeDtypeStruct((4, 4 * rows, features), BF16)
    sent_shape = jax.ShapeDtypeStruct((tokens, width // 2 + features), BF16)

    sent = call(send_kernel, [sent_shape], (place, activations, cotangent), 0, "send")[0]
    got = trade(sent, "core", 1)

    term = call(
        grad_kernel,
        [term_shape],
        (place, activations, cotangent, got),
        2 * tokens * width * features,
        "grad",
    )[0]
    come = exchange(term, "x")

    late_half = lax.optimization_barrier((weight_half, term))[0]
    near = [late_half] + [trade(late_half, "zh", k) for k in (1, 2, 3)]
    pair = add_other(lax.optimization_barrier((late_half, near[1]))[0], "y", 1)
    column = jnp.concatenate(near, axis=0)
    column, pair = lax.optimization_barrier((column, pair))
    halves = [column] + [trade(column, "x", j) for j in (1, 2, 3)]
    four = add_other(pair, "y", 2)
    eight = add_other(four, "y", 4)
    come, eight = lax.optimization_barrier((come, eight))
    part = total(come).astype(BF16)
    summed = add_other(eight, "zl", 1)

    grad_sum = total(exchange(part.reshape(4, rows, features), "zh"))
    grad = grad_sum * scale_factor

    flops = tokens * width * features

    def their_keys(*refs):
        keys_kernel(their_block, *refs)

    def our_keys(*refs):
        keys_kernel(own_block, *refs)

    halves = lax.optimization_barrier((*halves, part))[:4]
    away = call(their_keys, [keys_shape], (place, got, *halves), flops, "their_keys")[0]
    back = trade(away, "core", 1)
    keys = call(our_keys, [keys_shape], (place, activations, *halves), flops, "our_keys")[0]
    key_out = ((keys + back) * scale_factor).astype(BF16)

    replicas = lax.axis_size(REPLICA)
    new_first = 0.9 * first_moment[0] + 0.1 * grad
    new_second = 0.95 * second_moment[0] + 0.05 * grad * grad
    stepped = weight - 0.02 * (new_first / (jnp.sqrt(new_second) + 1e-08) + 0.1 * weight)
    new_anchor, new_momentum = outer_update(summed, anchor_weight, outer_momentum, replicas)
    new_weight = 0.5 * stepped + 0.5 * new_anchor
    return (key_out, new_weight[None], new_first[None], new_second[None], new_anchor, new_momentum)


def solution(mesh):
    fine = Mesh(mesh.devices.reshape(2, 8, 4, 4, 2), REPLICA + FSDP)
    split = P(REPLICA + FSDP, None)
    state = P(REPLICA, FSDP, None)
    shared = P(FSDP, None)
    return jax.shard_map(
        shards,
        mesh=fine,
        in_specs=(split, split, state, state, state, shared, shared),
        out_specs=(split, state, state, state, shared, shared),
        check_vma=False,
    )
```

```python
import jax
import jax.numpy as jnp
from jax import lax
from jax.experimental import pallas as pl
from jax.experimental.pallas import tpu as pltpu
from jax.sharding import Mesh, PartitionSpec as P

REPLICA = ("zl", "y")
FSDP = ("x", "zh", "core")
F32 = jnp.float32
BF16 = jnp.bfloat16
BLOCK = 128
SMEM = pl.BlockSpec(memory_space=pltpu.SMEM)
VMEM = pl.BlockSpec(memory_space=pltpu.VMEM)


def outer_update(summed, anchor_part, momentum_part, replicas):
    pseudo = anchor_part - summed * (1.0 / replicas)
    momentum_next = 0.9 * momentum_part + pseudo
    anchor_next = anchor_part - 0.7 * (pseudo + 0.9 * momentum_next)
    return (anchor_next, momentum_next)


def trade(block, axis, mask):
    return lax.ppermute(block, axis, [(i, i ^ mask) for i in range(lax.axis_size(axis))])


def add_other(value, axis, mask):
    held = value.astype(BF16)
    return held.astype(F32) + trade(held, axis, mask).astype(F32)


def exchange(blocks, axis):
    return lax.all_to_all(blocks, axis, 0, 0, tiled=True)


def total(blocks):
    return jnp.sum(blocks.astype(F32), axis=0)


def call(kernel, outs, args, flops, name, after=()):
    count = len(args)
    moved = sum(a.size * a.dtype.itemsize for a in args)

    def body(*refs):
        kernel(*refs[:count], *refs[count + len(after) :])

    return pl.pallas_call(
        body,
        in_specs=[SMEM] + [VMEM] * (count - 1) + [pl.BlockSpec(memory_space=pl.ANY)] * len(after),
        out_specs=[VMEM] * len(outs),
        out_shape=outs,
        cost_estimate=pl.CostEstimate(flops=flops, bytes_accessed=2 * moved, transcendentals=0),
        compiler_params=pltpu.CompilerParams(vmem_limit_bytes=24 * 2**20),
        name=name,
    )(*args, *after)


def send_kernel(place_ref, x_ref, c_ref, out_ref):
    width = x_ref.shape[1]

    def put(offset):
        for block in range(width // (2 * BLOCK)):
            at = 2 * BLOCK * block + offset
            out_ref[:, BLOCK * block : BLOCK * (block + 1)] = x_ref[:, at : at + BLOCK]

    pl.when(place_ref[0] == 0)(lambda: put(BLOCK))
    pl.when(place_ref[0] != 0)(lambda: put(0))
    out_ref[:, width // 2 :] = c_ref[...]


def own_block(core, x_ref, at):
    return x_ref[:, pl.ds(pl.multiple_of((2 * at + core) * BLOCK, BLOCK), BLOCK)]


def their_block(core, got_ref, at):
    return got_ref[:, pl.ds(pl.multiple_of(at * BLOCK, BLOCK), BLOCK)]


def four_blocks(pick, core, ref, j):
    return jnp.concatenate([pick(core, ref, 4 * j + k) for k in range(4)], axis=1)


def grad_kernel(place_ref, x_ref, c_ref, got_ref, out_ref):
    ours = c_ref[...]
    theirs = got_ref[:, got_ref.shape[1] - ours.shape[1] :]
    rows = (((0,), (0,)), ((), ()))
    for j in range(4):
        a = four_blocks(own_block, place_ref[0], x_ref, j)
        b = four_blocks(their_block, place_ref[0], got_ref, j)
        term = lax.dot_general(a, ours, rows, preferred_element_type=F32)
        term += lax.dot_general(b, theirs, rows, preferred_element_type=F32)
        out_ref[j] = term.astype(out_ref.dtype)


def keys_kernel(pick, place_ref, x_ref, *refs):
    out_ref = refs[-1]
    for j, w_ref in enumerate(refs[:-1]):
        group = 4 * (place_ref[1] ^ j)
        picked = [pick(place_ref[0], x_ref, group + (place_ref[2] ^ k)) for k in range(4)]
        a = jnp.concatenate(picked, axis=1)
        term = jnp.dot(a, w_ref[...], preferred_element_type=F32)
        out_ref[...] = term if j == 0 else out_ref[...] + term


def shards(
    activations, cotangent, local_weight, first_moment, second_moment, anchor_weight, outer_momentum
):
    tokens, width = activations.shape
    rows, features = anchor_weight.shape
    scale_factor = width ** (-0.5)
    weight = local_weight[0]
    weight_half = weight.astype(BF16)
    place = jnp.stack([lax.axis_index(a) for a in ("core", "x", "zh")]).astype(jnp.int32)
    keys_shape = jax.ShapeDtypeStruct((tokens, features), F32)
    term_shape = jax.ShapeDtypeStruct((4, 4 * rows, features), BF16)
    sent_shape = jax.ShapeDtypeStruct((tokens, width // 2 + features), BF16)

    sent = call(send_kernel, [sent_shape], (place, activations, cotangent), 0, "send")[0]
    got = trade(sent, "core", 1)

    term = call(
        grad_kernel,
        [term_shape],
        (place, activations, cotangent, got),
        2 * tokens * width * features,
        "grad",
    )[0]
    come = exchange(term, "x")

    late_half = lax.optimization_barrier((weight_half, term))[0]
    near = [late_half] + [trade(late_half, "zh", k) for k in (1, 2, 3)]
    pair = add_other(lax.optimization_barrier((late_half, near[1]))[0], "y", 1)
    column = jnp.concatenate(near, axis=0)
    column, pair = lax.optimization_barrier((column, pair))
    halves = [column] + [trade(column, "x", j) for j in (1, 2, 3)]
    four = add_other(pair, "y", 2)
    come, four = lax.optimization_barrier((come, four))
    part = total(come).astype(BF16)
    eight = add_other(four, "y", 4)
    summed = add_other(eight, "zl", 1)

    grad_sum = total(exchange(part.reshape(4, rows, features), "zh"))
    grad = grad_sum * scale_factor

    flops = tokens * width * features

    def their_keys(*refs):
        keys_kernel(their_block, *refs)

    def our_keys(*refs):
        keys_kernel(own_block, *refs)

    away = call(their_keys, [keys_shape], (place, got, *halves), flops, "their_keys", after=(part, eight))[0]
    back = trade(away, "core", 1)
    keys = call(our_keys, [keys_shape], (place, activations, *halves), flops, "our_keys")[0]
    key_out = ((keys + back) * scale_factor).astype(BF16)

    replicas = lax.axis_size(REPLICA)
    new_first = 0.9 * first_moment[0] + 0.1 * grad
    new_second = 0.95 * second_moment[0] + 0.05 * grad * grad
    stepped = weight - 0.02 * (new_first / (jnp.sqrt(new_second) + 1e-08) + 0.1 * weight)
    new_anchor, new_momentum = outer_update(summed, anchor_weight, outer_momentum, replicas)
    new_weight = 0.5 * stepped + 0.5 * new_anchor
    return (key_out, new_weight[None], new_first[None], new_second[None], new_anchor, new_momentum)


def solution(mesh):
    fine = Mesh(mesh.devices.reshape(2, 8, 4, 4, 2), REPLICA + FSDP)
    split = P(REPLICA + FSDP, None)
    state = P(REPLICA, FSDP, None)
    shared = P(FSDP, None)
    return jax.shard_map(
        shards,
        mesh=fine,
        in_specs=(split, split, state, state, state, shared, shared),
        out_specs=(split, state, state, state, shared, shared),
        check_vma=False,
    )
```

```python
import jax
import jax.numpy as jnp
from jax import lax
from jax.experimental import pallas as pl
from jax.experimental.pallas import tpu as pltpu
from jax.sharding import Mesh, PartitionSpec as P

REPLICA = ("zl", "y")
FSDP = ("x", "zh", "core")
F32 = jnp.float32
BF16 = jnp.bfloat16
BLOCK = 128
SMEM = pl.BlockSpec(memory_space=pltpu.SMEM)
VMEM = pl.BlockSpec(memory_space=pltpu.VMEM)


def outer_update(summed, anchor_part, momentum_part, replicas):
    pseudo = anchor_part - summed * (1.0 / replicas)
    momentum_next = 0.9 * momentum_part + pseudo
    anchor_next = anchor_part - 0.7 * (pseudo + 0.9 * momentum_next)
    return (anchor_next, momentum_next)


def trade(block, axis, mask):
    return lax.ppermute(block, axis, [(i, i ^ mask) for i in range(lax.axis_size(axis))])


def add_other(value, axis, mask):
    held = value.astype(BF16)
    return held.astype(F32) + trade(held, axis, mask).astype(F32)


def exchange(blocks, axis):
    return lax.all_to_all(blocks, axis, 0, 0, tiled=True)


def total(blocks):
    return jnp.sum(blocks.astype(F32), axis=0)


def call(kernel, outs, args, flops, name, after=()):
    count = len(args)
    moved = sum(a.size * a.dtype.itemsize for a in args)

    def body(*refs):
        kernel(*refs[:count], *refs[count + len(after) :])

    return pl.pallas_call(
        body,
        in_specs=[SMEM] + [VMEM] * (count - 1) + [pl.BlockSpec(memory_space=pl.ANY)] * len(after),
        out_specs=[VMEM] * len(outs),
        out_shape=outs,
        cost_estimate=pl.CostEstimate(flops=flops, bytes_accessed=2 * moved, transcendentals=0),
        compiler_params=pltpu.CompilerParams(vmem_limit_bytes=24 * 2**20),
        name=name,
    )(*args, *after)


def send_kernel(place_ref, x_ref, c_ref, out_ref):
    width = x_ref.shape[1]

    def put(offset):
        for block in range(width // (2 * BLOCK)):
            at = 2 * BLOCK * block + offset
            out_ref[:, BLOCK * block : BLOCK * (block + 1)] = x_ref[:, at : at + BLOCK]

    pl.when(place_ref[0] == 0)(lambda: put(BLOCK))
    pl.when(place_ref[0] != 0)(lambda: put(0))
    out_ref[:, width // 2 :] = c_ref[...]


def own_block(core, x_ref, at):
    return x_ref[:, pl.ds(pl.multiple_of((2 * at + core) * BLOCK, BLOCK), BLOCK)]


def their_block(core, got_ref, at):
    return got_ref[:, pl.ds(pl.multiple_of(at * BLOCK, BLOCK), BLOCK)]


def four_blocks(pick, core, ref, j):
    return jnp.concatenate([pick(core, ref, 4 * j + k) for k in range(4)], axis=1)


def grad_kernel(place_ref, x_ref, c_ref, got_ref, out_ref):
    ours = c_ref[...]
    theirs = got_ref[:, got_ref.shape[1] - ours.shape[1] :]
    rows = (((0,), (0,)), ((), ()))
    for j in range(4):
        a = four_blocks(own_block, place_ref[0], x_ref, j)
        b = four_blocks(their_block, place_ref[0], got_ref, j)
        term = lax.dot_general(a, ours, rows, preferred_element_type=F32)
        term += lax.dot_general(b, theirs, rows, preferred_element_type=F32)
        out_ref[j] = term.astype(out_ref.dtype)


def keys_kernel(pick, place_ref, x_ref, *refs):
    out_ref = refs[-1]
    for j, w_ref in enumerate(refs[:-1]):
        group = 4 * (place_ref[1] ^ j)
        picked = [pick(place_ref[0], x_ref, group + (place_ref[2] ^ k)) for k in range(4)]
        a = jnp.concatenate(picked, axis=1)
        term = jnp.dot(a, w_ref[...], preferred_element_type=F32)
        out_ref[...] = term if j == 0 else out_ref[...] + term


def shards(
    activations, cotangent, local_weight, first_moment, second_moment, anchor_weight, outer_momentum
):
    tokens, width = activations.shape
    rows, features = anchor_weight.shape
    scale_factor = width ** (-0.5)
    weight = local_weight[0]
    weight_half = weight.astype(BF16)
    place = jnp.stack([lax.axis_index(a) for a in ("core", "x", "zh")]).astype(jnp.int32)
    keys_shape = jax.ShapeDtypeStruct((tokens, features), F32)
    term_shape = jax.ShapeDtypeStruct((4, 4 * rows, features), BF16)
    sent_shape = jax.ShapeDtypeStruct((tokens, width // 2 + features), BF16)

    sent = call(send_kernel, [sent_shape], (place, activations, cotangent), 0, "send")[0]
    got = trade(sent, "core", 1)

    term = call(
        grad_kernel,
        [term_shape],
        (place, activations, cotangent, got),
        2 * tokens * width * features,
        "grad",
    )[0]
    come = exchange(term, "x")

    late_half = lax.optimization_barrier((weight_half, term))[0]
    near = [late_half] + [trade(late_half, "zh", k) for k in (1, 2, 3)]
    own = lax.optimization_barrier((late_half, near[1]))[0]
    others = [trade(own, "y", mask) for mask in (1, 2, 3)]
    column = jnp.concatenate(near, axis=0)
    column, others[0] = lax.optimization_barrier((column, others[0]))
    halves = [column] + [trade(column, "x", j) for j in (1, 2, 3)]
    wide = [value.astype(F32) for value in (own, *others)]
    four = (wide[0] + wide[1]) + (wide[2] + wide[3])
    come, four = lax.optimization_barrier((come, four))
    part = total(come).astype(BF16)
    eight = add_other(four, "y", 4)
    summed = add_other(eight, "zl", 1)

    grad_sum = total(exchange(part.reshape(4, rows, features), "zh"))
    grad = grad_sum * scale_factor

    flops = tokens * width * features

    def their_keys(*refs):
        keys_kernel(their_block, *refs)

    def our_keys(*refs):
        keys_kernel(own_block, *refs)

    away = call(their_keys, [keys_shape], (place, got, *halves), flops, "their_keys", after=(part, eight))[0]
    back = trade(away, "core", 1)
    keys = call(our_keys, [keys_shape], (place, activations, *halves), flops, "our_keys")[0]
    key_out = ((keys + back) * scale_factor).astype(BF16)

    replicas = lax.axis_size(REPLICA)
    new_first = 0.9 * first_moment[0] + 0.1 * grad
    new_second = 0.95 * second_moment[0] + 0.05 * grad * grad
    stepped = weight - 0.02 * (new_first / (jnp.sqrt(new_second) + 1e-08) + 0.1 * weight)
    new_anchor, new_momentum = outer_update(summed, anchor_weight, outer_momentum, replicas)
    new_weight = 0.5 * stepped + 0.5 * new_anchor
    return (key_out, new_weight[None], new_first[None], new_second[None], new_anchor, new_momentum)


def solution(mesh):
    fine = Mesh(mesh.devices.reshape(2, 8, 4, 4, 2), REPLICA + FSDP)
    split = P(REPLICA + FSDP, None)
    state = P(REPLICA, FSDP, None)
    shared = P(FSDP, None)
    return jax.shard_map(
        shards,
        mesh=fine,
        in_specs=(split, split, state, state, state, shared, shared),
        out_specs=(split, state, state, state, shared, shared),
        check_vma=False,
    )
```

```python
import jax
import jax.numpy as jnp
from jax import lax
from jax.experimental import pallas as pl
from jax.experimental.pallas import tpu as pltpu
from jax.sharding import Mesh, PartitionSpec as P

REPLICA = ("zl", "y")
FSDP = ("x", "zh", "core")
F32 = jnp.float32
BF16 = jnp.bfloat16
BLOCK = 128
SMEM = pl.BlockSpec(memory_space=pltpu.SMEM)
VMEM = pl.BlockSpec(memory_space=pltpu.VMEM)


def outer_update(summed, anchor_part, momentum_part, replicas):
    pseudo = anchor_part - summed * (1.0 / replicas)
    momentum_next = 0.9 * momentum_part + pseudo
    anchor_next = anchor_part - 0.7 * (pseudo + 0.9 * momentum_next)
    return (anchor_next, momentum_next)


def trade(block, axis, mask):
    return lax.ppermute(block, axis, [(i, i ^ mask) for i in range(lax.axis_size(axis))])


def add_other(value, axis, mask):
    held = value.astype(BF16)
    return held.astype(F32) + trade(held, axis, mask).astype(F32)


def exchange(blocks, axis):
    return lax.all_to_all(blocks, axis, 0, 0, tiled=True)


def total(blocks):
    return jnp.sum(blocks.astype(F32), axis=0)


def call(kernel, outs, args, flops, name, after=()):
    count = len(args)
    moved = sum(a.size * a.dtype.itemsize for a in args)

    def body(*refs):
        kernel(*refs[:count], *refs[count + len(after) :])

    return pl.pallas_call(
        body,
        in_specs=[SMEM] + [VMEM] * (count - 1) + [pl.BlockSpec(memory_space=pl.ANY)] * len(after),
        out_specs=[VMEM] * len(outs),
        out_shape=outs,
        cost_estimate=pl.CostEstimate(flops=flops, bytes_accessed=2 * moved, transcendentals=0),
        compiler_params=pltpu.CompilerParams(vmem_limit_bytes=24 * 2**20),
        name=name,
    )(*args, *after)


def send_kernel(place_ref, x_ref, c_ref, out_ref):
    width = x_ref.shape[1]

    def put(offset):
        for block in range(width // (2 * BLOCK)):
            at = 2 * BLOCK * block + offset
            out_ref[:, BLOCK * block : BLOCK * (block + 1)] = x_ref[:, at : at + BLOCK]

    pl.when(place_ref[0] == 0)(lambda: put(BLOCK))
    pl.when(place_ref[0] != 0)(lambda: put(0))
    out_ref[:, width // 2 :] = c_ref[...]


def own_block(core, x_ref, at):
    return x_ref[:, pl.ds(pl.multiple_of((2 * at + core) * BLOCK, BLOCK), BLOCK)]


def their_block(core, got_ref, at):
    return got_ref[:, pl.ds(pl.multiple_of(at * BLOCK, BLOCK), BLOCK)]


def four_blocks(pick, core, ref, j):
    return jnp.concatenate([pick(core, ref, 4 * j + k) for k in range(4)], axis=1)


def grad_kernel(place_ref, x_ref, c_ref, got_ref, out_ref):
    ours = c_ref[...]
    theirs = got_ref[:, got_ref.shape[1] - ours.shape[1] :]
    rows = (((0,), (0,)), ((), ()))
    for j in range(4):
        a = four_blocks(own_block, place_ref[0], x_ref, j)
        b = four_blocks(their_block, place_ref[0], got_ref, j)
        term = lax.dot_general(a, ours, rows, preferred_element_type=F32)
        term += lax.dot_general(b, theirs, rows, preferred_element_type=F32)
        out_ref[j] = term.astype(out_ref.dtype)


def keys_kernel(pick, place_ref, x_ref, *refs):
    out_ref = refs[-1]
    for j, w_ref in enumerate(refs[:-1]):
        group = 4 * (place_ref[1] ^ j)
        picked = [pick(place_ref[0], x_ref, group + (place_ref[2] ^ k)) for k in range(4)]
        a = jnp.concatenate(picked, axis=1)
        term = jnp.dot(a, w_ref[...], preferred_element_type=F32)
        out_ref[...] = term if j == 0 else out_ref[...] + term


def shards(
    activations, cotangent, local_weight, first_moment, second_moment, anchor_weight, outer_momentum
):
    tokens, width = activations.shape
    rows, features = anchor_weight.shape
    scale_factor = width ** (-0.5)
    weight = local_weight[0]
    weight_half = weight.astype(BF16)
    place = jnp.stack([lax.axis_index(a) for a in ("core", "x", "zh")]).astype(jnp.int32)
    keys_shape = jax.ShapeDtypeStruct((tokens, features), F32)
    term_shape = jax.ShapeDtypeStruct((4, 4 * rows, features), BF16)
    sent_shape = jax.ShapeDtypeStruct((tokens, width // 2 + features), BF16)

    sent = call(send_kernel, [sent_shape], (place, activations, cotangent), 0, "send")[0]
    got = trade(sent, "core", 1)

    term = call(
        grad_kernel,
        [term_shape],
        (place, activations, cotangent, got),
        2 * tokens * width * features,
        "grad",
    )[0]
    come = exchange(term, "x")

    late_half = lax.optimization_barrier((weight_half, term))[0]
    near = [late_half] + [trade(late_half, "zh", k) for k in (1, 2, 3)]
    own = lax.optimization_barrier((late_half, near[1]))[0]
    others = [trade(own, "y", mask) for mask in (1, 2, 3)]
    column = jnp.concatenate(near, axis=0)
    column, others[0] = lax.optimization_barrier((column, others[0]))
    halves = [column] + [trade(column, "x", j) for j in (1, 2, 3)]
    wide = [value.astype(F32) for value in (own, *others)]
    four = (wide[0] + wide[1]) + (wide[2] + wide[3])
    come, four = lax.optimization_barrier((come, four))
    part = total(come).astype(BF16)
    four, part = lax.optimization_barrier((four, part))
    eight = add_other(four, "y", 4)
    summed = add_other(eight, "zl", 1)

    grad_sum = total(exchange(part.reshape(4, rows, features), "zh"))
    grad = grad_sum * scale_factor

    flops = tokens * width * features

    def their_keys(*refs):
        keys_kernel(their_block, *refs)

    def our_keys(*refs):
        keys_kernel(own_block, *refs)

    away = call(their_keys, [keys_shape], (place, got, *halves), flops, "their_keys", after=(part, eight))[0]
    back = trade(away, "core", 1)
    keys = call(our_keys, [keys_shape], (place, activations, *halves), flops, "our_keys")[0]
    key_out = ((keys + back) * scale_factor).astype(BF16)

    replicas = lax.axis_size(REPLICA)
    new_first = 0.9 * first_moment[0] + 0.1 * grad
    new_second = 0.95 * second_moment[0] + 0.05 * grad * grad
    stepped = weight - 0.02 * (new_first / (jnp.sqrt(new_second) + 1e-08) + 0.1 * weight)
    new_anchor, new_momentum = outer_update(summed, anchor_weight, outer_momentum, replicas)
    new_weight = 0.5 * stepped + 0.5 * new_anchor
    return (key_out, new_weight[None], new_first[None], new_second[None], new_anchor, new_momentum)


def solution(mesh):
    fine = Mesh(mesh.devices.reshape(2, 8, 4, 4, 2), REPLICA + FSDP)
    split = P(REPLICA + FSDP, None)
    state = P(REPLICA, FSDP, None)
    shared = P(FSDP, None)
    return jax.shard_map(
        shards,
        mesh=fine,
        in_specs=(split, split, state, state, state, shared, shared),
        out_specs=(split, state, state, state, shared, shared),
        check_vma=False,
    )
```
